128 devices in a mesh: group: 4 (over z), member: 32 (over y, x, core).
Axes of the slice: x: 4, y: 4, z: 4, core: 2. Of those that a mesh axis runs over, the one named last changes fastest.
Arguments:
- history: bfloat16 [65536, 64, 128], P(('group', 'member')), may hold values from -6 to 6
- near_time: bfloat16 [8, 64], replicated, may hold values from -0.75 to 0.75
- near_kernel: bfloat16 [8, 128, 128], replicated, may hold values from -0.1875 to 0.1875
- projection: bfloat16 [64, 128, 256], replicated, may hold values from -0.0625 to 0.0625
- receive_map: bfloat16 [256, 128], replicated, may hold values from -0.375 to 0.375
- self_inverse: bfloat16 [128, 128], replicated, may hold values from -0.5 to 0.5
- incident: float32 [2, 65536, 128], P(None, ('group', 'member')), may hold values from -6 to 6
- neighbours: int32 [65536, 8], P(('group', 'member')), may hold values from 0 to 65535, as said below
- send_sources: int32 [128, 128, 2], P(('group', 'member')), may hold values from -1 to 511, as said below
- recv_observers: int32 [128, 128, 2], P(('group', 'member')), may hold values from -1 to 511, as said below
- transfer: bfloat16 [128, 128, 2, 256], P(('group', 'member')), may hold values from -6 to 6
Outputs:
- currents: float32 [2, 65536, 128], P(None, ('group', 'member'))
The draws below stay inside these ranges and needn't reach their ends.
Inputs may be any that keep to these rules, and one draw needn't show every extreme that they name: `neighbours`: every neighbour lies in the cluster's own group of 16384 consecutive clusters, at most 32 clusters from the cluster; the first slot lies 32 clusters away unless the group ends first. `send_sources`: entry [a, b, s] is a cluster of device a, numbered 0 to 511, whose rays device b needs in slot s, or -1 for an empty slot; used slots come first; devices of one group send each other nothing; some pair of devices fills all 2 slots. `recv_observers`: entry [b, a, s] is a cluster of device b, numbered 0 to 511, observing what device a sends in slot s; it is -1 exactly where send_sources[a, b, s] is -1.
All inputs are finite; a program needn't handle non-finite values.
Results may differ from the reference program's by a relative error of at most 0.0038.
Values may be sent and summed in bfloat16 or wider, within the bound.
A program may use at most 64 MiB of HBM per device.

```python
import jax
import jax.numpy as jnp
from jax import lax

CL_DEV = 512
NB = 128
H = 64
K = 256
NNB = 8
CAP = 2
STEPS = 2
RIM = 32
CLUSTERS = 65536
GROUP_CLUSTERS = 16384
DEVICES = 128


def pair_tables(key):
    count_key, busy_key, source_key, observer_key = jax.random.split(key, 4)
    counts = jnp.minimum(jax.random.randint(count_key, (DEVICES, DEVICES), 0, CAP + 2), CAP)
    busy = jax.random.randint(busy_key, (DEVICES,), 0, 4) == 0
    counts = jnp.where(busy[:, None], CAP, counts)
    group_of = jnp.arange(DEVICES, dtype=jnp.int32) // (GROUP_CLUSTERS // CL_DEV)
    counts = jnp.where(group_of[:, None] == group_of[None, :], 0, counts)
    slot_ids = jnp.arange(CAP, dtype=jnp.int32)
    occupied = slot_ids[None, None, :] < counts[:, :, None]
    sources = jax.random.randint(source_key, (DEVICES, DEVICES, CAP), 0, CL_DEV)
    observers = jax.random.randint(observer_key, (DEVICES, DEVICES, CAP), 0, CL_DEV)
    return (jnp.where(occupied, sources, -1), jnp.where(occupied, observers, -1))


def draw_send_sources(key, part):
    sources, observers = pair_tables(key)
    return sources.astype(jnp.int32)


def draw_recv_observers(key, part):
    sources, observers = pair_tables(key)
    return jnp.transpose(observers, (1, 0, 2)).astype(jnp.int32)


def draw_neighbours(key, part):
    key = jax.random.fold_in(key, 5)
    offset_key, sign_key = jax.random.split(key, 2)
    own_cluster = jnp.arange(CLUSTERS, dtype=jnp.int32)[:, None]
    offsets = jax.random.randint(offset_key, (CLUSTERS, NNB), -RIM, RIM + 1)
    signs = jax.random.randint(sign_key, (CLUSTERS,), 0, 2) * 2 - 1
    offsets = offsets.at[:, 0].set(signs * RIM)
    group_start = own_cluster // GROUP_CLUSTERS * GROUP_CLUSTERS
    return jnp.clip(own_cluster + offsets, group_start, group_start + GROUP_CLUSTERS - 1).astype(jnp.int32)


def steps_of(rng, dims, cuts, low, largest):
    level, own = 1.0, jax.random.fold_in(rng, 6)
    for dim, shards_of in cuts:
        draws = jnp.exp(jax.random.uniform(jax.random.fold_in(own, dim), (shards_of,), jnp.float32, low / len(cuts), largest / len(cuts)))
        level = level * jnp.repeat(draws, dims[dim] // shards_of).reshape([-1 if axis == dim else 1 for axis in range(len(dims))])
    return level


def noise(stream_key, extent, scale, limit, cuts=(), kind=jnp.bfloat16):
    drawn = jax.random.normal(stream_key, extent, jnp.float32) * scale
    if len(cuts) > 0:
        drawn = steps_of(stream_key, extent, cuts, -0.22, 0.18) * drawn
    return jnp.clip(drawn, min=-limit, max=limit).astype(kind)


def setup_inputs(seed: int = 0) -> dict:
    key_list = jax.random.split(jax.random.key(seed), 12)
    return {
        "history": noise(key_list[0], (CLUSTERS, H, NB), 1.0, 6.0, ((0, 128),)),
        "near_time": noise(key_list[1], (NNB, H), H ** -0.5, 0.75),
        "near_kernel": noise(key_list[2], (NNB, NB, NB), (NNB * NB) ** -0.5, 0.1875),
        "projection": noise(key_list[3], (H, NB, K), (H * NB) ** -0.5, 0.0625),
        "receive_map": noise(key_list[4], (K, NB), K ** -0.5, 0.375),
        "self_inverse": noise(key_list[5], (NB, NB), NB ** -0.5, 0.5),
        "incident": noise(key_list[6], (STEPS, CLUSTERS, NB), 1.0, 6.0, ((1, 128),), jnp.float32),
        "neighbours": draw_neighbours(jax.random.fold_in(key_list[11], 71), 0),
        "send_sources": draw_send_sources(jax.random.fold_in(key_list[11], 71), 0),
        "recv_observers": draw_recv_observers(jax.random.fold_in(key_list[11], 71), 0),
        "transfer": noise(key_list[10], (DEVICES, DEVICES, CAP, K), 1.0, 6.0, ((0, 128),)),
    }


def reference(history, near_time, near_kernel, projection, receive_map, self_inverse, incident, neighbours, send_sources, recv_observers, transfer):
    kernel_flat = near_kernel.reshape(NNB * NB, NB)
    projection_flat = projection.reshape(H * NB, K)
    time_weights = near_time.astype(jnp.float32)
    device_base = jnp.arange(DEVICES, dtype=jnp.int32) * CL_DEV
    source_table = jnp.transpose(send_sources, (1, 0, 2))
    occupied = recv_observers >= 0
    source_global = device_base[None, :, None] + jnp.maximum(source_table, 0)
    observer_global = jnp.where(occupied, device_base[:, None, None] + recv_observers, CLUSTERS).astype(jnp.int32)
    index_table = jnp.broadcast_to(neighbours[:, :, None], (CLUSTERS, NNB, NB))
    results = []
    for time_step in range(STEPS):
        def per_block(block):
            reduced_block = jnp.einsum('jh,shb->sjb', time_weights, block.astype(jnp.float32)).astype(jnp.bfloat16)
            outgoing_block = jnp.dot(block.reshape(CL_DEV, H * NB), projection_flat, preferred_element_type=jnp.float32).astype(jnp.bfloat16)
            return reduced_block, outgoing_block
        reduced, outgoing = lax.map(per_block, history.reshape(DEVICES, CL_DEV, H, NB))
        reduced = reduced.reshape(CLUSTERS, NNB, NB)
        outgoing = outgoing.reshape(CLUSTERS, K)
        picked = jnp.take_along_axis(reduced, index_table, axis=0)
        near_field = jnp.dot(picked.reshape(CLUSTERS, NNB * NB), kernel_flat, preferred_element_type=jnp.float32)
        values = outgoing[source_global].astype(jnp.float32)
        contributions = jnp.where(occupied[..., None], transfer.astype(jnp.float32) * values, 0.0)
        incoming = jax.ops.segment_sum(contributions.reshape(-1, K), observer_global.reshape(-1), num_segments=CLUSTERS + 1)[:CLUSTERS].astype(jnp.bfloat16)
        far_field = jnp.dot(incoming, receive_map, preferred_element_type=jnp.float32)
        right_side = (incident[time_step] - near_field - far_field).astype(jnp.bfloat16)
        current = jnp.dot(right_side, self_inverse, preferred_element_type=jnp.float32)
        results.append(current)
        history = jnp.concatenate([current.astype(jnp.bfloat16)[:, None], history[:, :H - 1]], axis=1)
    return jnp.stack(results)
```

```python
import functools

import jax
import jax.numpy as jnp
from jax import lax
from jax.experimental import pallas as pl
from jax.experimental.pallas import tpu as pltpu
from jax.sharding import PartitionSpec as P

MESH = pl.DeviceIdType.MESH
BF16 = jnp.bfloat16
F32 = jnp.float32

CL = 512
NB = 128
H = 64
K = 256
NNB = 8
RIM = 32
GROUPS = 4
MEMBERS = 32
HC = 16
NQ = H // HC
ROWS = 3 * MEMBERS * 2
PAIRS = GROUPS * MEMBERS * 2
EXT = CL + 2 * RIM
BLK = 128
WIN = BLK + 2 * RIM


def dot(a, b):
    return jnp.dot(a, b, preferred_element_type=F32)


def iota(shape, dim):
    return lax.broadcasted_iota(jnp.int32, shape, dim)


def one_hot(mask):
    return jnp.where(mask, 1.0, 0.0).astype(BF16)


def far_offsets():
    dist = (0, 1, 2, 1)
    offsets = [
        (dz, dy, dx, dc) for dz in (2, 1, 3) for dy in range(4) for dx in range(4) for dc in (1, 0)
    ]
    return sorted(offsets, key=lambda o: -(dist[o[0]] + dist[o[1]] + dist[o[2]]))


def kernel(
    src_hbm,
    obs_hbm,
    hist_hbm,
    ntime_hbm,
    nkern_hbm,
    proj_hbm,
    rmap_hbm,
    sinv_hbm,
    inc_hbm,
    nbr_hbm,
    trans_hbm,
    out_hbm,
    src,
    obs,
    hv0,
    hv1,
    hv2,
    hv3,
    ntime,
    nkern,
    pv,
    rmap,
    sinv,
    inc,
    nbr,
    trans,
    cur,
    arows,
    part1,
    perm,
    gone,
    oone,
    sone,
    mone,
    tt,
    rext,
    r1p,
    base,
    outb,
    inb,
    load_sem,
    hist_sem,
    proj_sem,
    send_sem,
    recv_sem,
    halo_send,
    halo_recv,
    out_sem,
):
    g = lax.axis_index("group")
    m = lax.axis_index("member")
    me = g * MEMBERS + m
    z, y, x, c = g, m // 8, (m // 2) % 4, m % 2
    right = (m + 1) % MEMBERS
    left = (m + MEMBERS - 1) % MEMBERS

    def peer(o):
        dz, dy, dx, dc = o
        return (z + dz) % 4, ((y + dy) % 4) * 8 + ((x + dx) % 4) * 2 + (c + dc) % 2

    hv = (hv0, hv1, hv2, hv3)

    small = []

    def load(i, a, b):
        cp = pltpu.make_async_copy(a, b, load_sem.at[i])
        cp.start()
        small.append(cp)

    load(0, src_hbm, src)
    load(1, obs_hbm, obs)
    load(2, nbr_hbm, nbr)
    load(3, ntime_hbm, ntime)
    hist_cp = []
    proj_cp = []
    for q in range(NQ):
        cp = pltpu.make_async_copy(hist_hbm.at[:, pl.ds(q * HC, HC)], hv[q], hist_sem.at[q])
        cp.start()
        hist_cp.append(cp)
        cp = pltpu.make_async_copy(
            proj_hbm.at[pl.ds(q * HC * NB, HC * NB)], pv.at[pl.ds(q * HC * NB, HC * NB)], proj_sem.at[q]
        )
        cp.start()
        proj_cp.append(cp)
    load(4, nkern_hbm, nkern)
    load(5, inc_hbm, inc)
    load(6, trans_hbm, trans)
    load(7, rmap_hbm, rmap)
    load(8, sinv_hbm, sinv)

    barrier = pltpu.get_barrier_semaphore()
    for o in far_offsets():
        pl.semaphore_signal(barrier, inc=1, device_id=peer(o), device_id_type=MESH)
    pl.semaphore_signal(barrier, inc=1, device_id=(g, right), device_id_type=MESH)
    pl.semaphore_signal(barrier, inc=1, device_id=(g, left), device_id_type=MESH)

    r = iota((256, 256), 0)
    perm[...] = one_hot(iota((256, 256), 1) == (r % 16) * 16 + r // 16)
    for t in range(2):
        inb[t, :, pl.ds(g * MEMBERS, MEMBERS)] = jnp.zeros((2, MEMBERS, 2, 128), BF16)
    for cp in small[:4]:
        cp.wait()

    tn = ntime[...]
    rr = iota((128, NNB), 0)
    pick = one_hot((rr // 8) % 8 == iota((128, NNB), 1))
    wide = dot(pick, tn).astype(BF16)
    cols = iota((H, 512), 1)
    step = (cols // 128) * 16 + cols % 16
    same = one_hot(iota((H, 512), 0) == step)
    shifted = one_hot(iota((H, 512), 0) == step + 1)
    tr = iota((128, 512), 0)
    tc = iota((128, 512), 1)
    keep = tr % 8 == (tc // 16) % 8
    table = jnp.where(tr < 64, dot(wide, same), dot(wide, shifted))
    tt[...] = jnp.where(keep, table, 0.0).astype(BF16)

    oone[...] = one_hot(iota((CL, PAIRS), 0) == obs[...])
    sub = iota((8, CL), 0)
    lane = iota((8, CL), 1)

    def source_rows(i, carry):
        d = i // 8
        first = ((g + d + 1) % GROUPS) * 64 + (i % 8) * 8
        want = jnp.full((8, CL), -1, jnp.int32)
        for k in range(8):
            want = jnp.where(sub == k, src[first + k], want)
        sone[pl.ds(pl.multiple_of(i * 8, 8), 8), :] = jnp.where(lane == want, 1.0, 0.0)
        return carry

    lax.fori_loop(0, ROWS // 8, source_rows, 0)

    wl = iota((BLK, WIN), 1)
    for blk in range(CL // BLK):
        off = me * CL + blk * BLK - RIM
        for j in range(NNB):
            col = nbr[pl.ds(blk * BLK, BLK), j : j + 1] - off
            gone[blk, j] = one_hot(wl == col)

    acc = jnp.zeros((ROWS, K), F32)
    for q in range(NQ):
        hist_cp[q].wait()

        def gather(i, carry):
            d = i // 2
            first = ((g + d + 1) % GROUPS) * 64 + (i % 2) * 32
            parts = [hv[q][jnp.maximum(src[first + k], 0)] for k in range(32)]
            tile = jnp.concatenate(
                [jnp.concatenate(parts[:16], axis=0), jnp.concatenate(parts[16:], axis=0)], axis=1
            )
            turned = dot(perm[...], tile).astype(BF16)
            for h in range(HC):
                for s in range(2):
                    arows[
                        pl.ds(pl.multiple_of(i * 32 + s * 16, 16), 16), pl.ds((q * HC + h) * NB, NB)
                    ] = turned[h * 16 : (h + 1) * 16, s * NB : (s + 1) * NB]
            return carry

        lax.fori_loop(0, ROWS // 32, gather, 0)
        proj_cp[q].wait()
        acc = acc + dot(
            arows[:, pl.ds(q * HC * NB, HC * NB)], pv[pl.ds(q * HC * NB, HC * NB), :]
        )

    def store_rays(t, rows):
        flat = outb.at[t].reshape(2, ROWS, 128)
        flat[0] = rows[:, :NB]
        flat[1] = rows[:, NB:]

    def send_rays(t):
        for o in far_offsets():
            gg, mm = peer(o)
            pltpu.make_async_remote_copy(
                outb.at[t, :, (o[0] - 1) * MEMBERS + mm],
                inb.at[t, :, me],
                send_sem.at[t],
                recv_sem.at[t],
                device_id=(gg, mm),
                device_id_type=MESH,
            ).start()

    def wait_rays(t):
        part = inb.at[t, :, pl.ds(0, ROWS // 2)]
        pltpu.make_async_copy(part, part, recv_sem.at[t]).wait()

    def halo(t, side):
        if side == 0:
            return pltpu.make_async_remote_copy(
                rext.at[t, :, pl.ds(CL, RIM)],
                rext.at[t, :, pl.ds(0, RIM)],
                halo_send.at[t, 0],
                halo_recv.at[t, 0],
                device_id=(g, right),
                device_id_type=MESH,
            )
        return pltpu.make_async_remote_copy(
            rext.at[t, :, pl.ds(RIM, RIM)],
            rext.at[t, :, pl.ds(RIM + CL, RIM)],
            halo_send.at[t, 1],
            halo_recv.at[t, 1],
            device_id=(g, left),
            device_id_type=MESH,
        )

    outgoing = acc.astype(BF16)
    store_rays(0, outgoing)
    pl.semaphore_wait(barrier, 3 * MEMBERS + 2)
    send_rays(0)

    def reduce_group(i, carry):
        halves = []
        for s in range(2):
            first = pl.multiple_of(i * 16 + s * 8, 8)
            halves.append(
                jnp.concatenate([hv[q][pl.ds(first, 8)].reshape(128, NB) for q in range(NQ)], axis=0)
            )
        red = dot(tt[...], jnp.concatenate(halves, axis=1))
        at = pl.multiple_of(i * 16, 16)
        for j in range(NNB):
            a = red[j * 8 : j * 8 + 8]
            rext[0, j, pl.ds(pl.multiple_of(at + RIM, 16), 16), :] = jnp.concatenate(
                [a[:, :NB], a[:, NB:]], axis=0
            ).astype(BF16)
            b = red[64 + j * 8 : 72 + j * 8]
            r1p[j, pl.ds(at, 16), :] = jnp.concatenate([b[:, :NB], b[:, NB:]], axis=0)
        return carry

    for i in (0, 1, 30, 31):
        reduce_group(i, 0)
    halo(0, 0).start()
    halo(0, 1).start()
    lax.fori_loop(2, 30, reduce_group, 0)

    part1[...] = dot(arows[:, : (H - 1) * NB], pv[NB:, :])
    mone[...] = dot(sone[...].astype(BF16), oone[...]).astype(BF16)

    for cp in small[4:]:
        cp.wait()

    def near_block(t, blk):
        picked = [
            dot(gone[blk, j], rext[t, j, pl.ds(blk * BLK, WIN), :]).astype(BF16) for j in range(NNB)
        ]
        near = dot(jnp.concatenate(picked, axis=1), nkern[...])
        base[pl.ds(blk * BLK, BLK), :] = inc[t, pl.ds(blk * BLK, BLK), :] - near

    def near_field(t):
        near_block(t, 1)
        near_block(t, 2)
        halo(t, 0).wait_recv()
        near_block(t, 0)
        halo(t, 1).wait_recv()
        near_block(t, 3)

    def contributions(t):
        halves = [trans[s].astype(F32) * inb.at[t].reshape(2, PAIRS, 128)[s].astype(F32) for s in range(2)]
        full = jnp.concatenate(halves, axis=1)
        high = full.astype(BF16)
        low = (full - high.astype(F32)).astype(BF16)
        return high, low

    near_field(0)
    full = base[...]
    b0 = full.astype(BF16)
    rest = full - b0.astype(F32)
    b1 = rest.astype(BF16)
    b2 = (rest - b1.astype(F32)).astype(BF16)
    sel = sone[...].astype(BF16)
    base_src = dot(sel, b0) + dot(sel, b1) + dot(sel, b2)

    wait_rays(0)
    high, low = contributions(0)

    def currents(hot, start):
        incoming = (dot(hot, high) + dot(hot, low)).astype(BF16)
        rhs = (start - dot(incoming, rmap[...])).astype(BF16)
        return dot(rhs, sinv[...])

    at_src = currents(mone[...], base_src).astype(BF16)
    outgoing = (part1[...] + dot(at_src, pv[:NB, :])).astype(BF16)
    store_rays(1, outgoing)
    send_rays(1)

    cur0 = currents(oone[...], base[...])
    cur[0] = cur0
    out0 = pltpu.make_async_copy(cur.at[0], out_hbm.at[0], out_sem.at[0])
    out0.start()
    newest = cur0.astype(BF16).astype(F32)
    for j in range(NNB):
        weight = ntime[j : j + 1, 0:1].astype(F32)
        rext[1, j, pl.ds(RIM, CL), :] = (r1p[j] + weight * newest).astype(BF16)
    halo(1, 0).start()
    halo(1, 1).start()
    near_field(1)

    wait_rays(1)
    high, low = contributions(1)
    cur[1] = currents(oone[...], base[...])
    out1 = pltpu.make_async_copy(cur.at[1], out_hbm.at[1], out_sem.at[1])
    out1.start()
    for t in range(2):
        halo(t, 0).wait_send()
        halo(t, 1).wait_send()
        pltpu.make_async_copy(outb.at[t], outb.at[t], send_sem.at[t]).wait()
    out0.wait()
    out1.wait()


def body(
    history,
    near_time,
    near_kernel,
    projection,
    receive_map,
    self_inverse,
    incident,
    neighbours,
    send_sources,
    recv_observers,
    transfer,
):
    halves = transfer.reshape(PAIRS, 2, 128).swapaxes(0, 1)
    args = (
        send_sources.reshape(PAIRS),
        recv_observers.reshape(1, PAIRS),
        history,
        near_time,
        near_kernel.reshape(NNB * NB, NB),
        projection.reshape(H * NB, K),
        receive_map,
        self_inverse,
        incident,
        neighbours,
        halves,
    )
    scratch = [
        pltpu.SMEM((PAIRS,), jnp.int32),
        pltpu.VMEM((1, PAIRS), jnp.int32),
        *[pltpu.VMEM((CL, HC, NB), BF16) for _ in range(NQ)],
        pltpu.VMEM((NNB, H), BF16),
        pltpu.VMEM((NNB * NB, NB), BF16),
        pltpu.VMEM((H * NB, K), BF16),
        pltpu.VMEM((K, NB), BF16),
        pltpu.VMEM((NB, NB), BF16),
        pltpu.VMEM((2, CL, NB), F32),
        pltpu.VMEM((CL, NNB), jnp.int32),
        pltpu.VMEM((2, PAIRS, 128), BF16),
        pltpu.VMEM((2, CL, NB), F32),
        pltpu.VMEM((ROWS, H * NB), BF16),
        pltpu.VMEM((ROWS, K), F32),
        pltpu.VMEM((256, 256), BF16),
        pltpu.VMEM((CL // BLK, NNB, BLK, WIN), BF16),
        pltpu.VMEM((CL, PAIRS), BF16),
        pltpu.VMEM((ROWS, CL), F32),
        pltpu.VMEM((ROWS, PAIRS), BF16),
        pltpu.VMEM((128, 512), BF16),
        pltpu.VMEM((2, NNB, EXT, NB), BF16),
        pltpu.VMEM((NNB, CL, NB), F32),
        pltpu.VMEM((CL, NB), F32),
        pltpu.VMEM((2, 2, ROWS // 2, 2, 128), BF16),
        pltpu.VMEM((2, 2, PAIRS // 2, 2, 128), BF16),
        pltpu.SemaphoreType.DMA((9,)),
        pltpu.SemaphoreType.DMA((NQ,)),
        pltpu.SemaphoreType.DMA((NQ,)),
        pltpu.SemaphoreType.DMA((2,)),
        pltpu.SemaphoreType.DMA((2,)),
        pltpu.SemaphoreType.DMA((2, 2)),
        pltpu.SemaphoreType.DMA((2, 2)),
        pltpu.SemaphoreType.DMA((2,)),
    ]
    return pl.pallas_call(
        kernel,
        out_shape=jax.ShapeDtypeStruct((2, CL, NB), F32),
        in_specs=[pl.BlockSpec(memory_space=pl.ANY)] * len(args),
        out_specs=pl.BlockSpec(memory_space=pl.ANY),
        scratch_shapes=scratch,
        compiler_params=pltpu.CompilerParams(
            collective_id=0, has_side_effects=True, vmem_limit_bytes=50 << 20
        ),
        cost_estimate=pl.CostEstimate(
            flops=4_000_000_000, bytes_accessed=14 << 20, transcendentals=0
        ),
    )(*args)


def solution(mesh):
    both = ("group", "member")
    in_specs = (
        P(both, None, None),
        P(),
        P(),
        P(),
        P(),
        P(),
        P(None, both, None),
        P(both, None),
        P(both, None, None),
        P(both, None, None),
        P(both, None, None, None),
    )
    out_specs = P(None, both, None)
    return jax.shard_map(body, mesh=mesh, in_specs=in_specs, out_specs=out_specs, check_vma=False)
```

```python
import functools

import jax
import jax.numpy as jnp
from jax import lax
from jax.experimental import pallas as pl
from jax.experimental.pallas import tpu as pltpu
from jax.sharding import PartitionSpec as P

MESH = pl.DeviceIdType.MESH
BF16 = jnp.bfloat16
F32 = jnp.float32

CL = 512
NB = 128
H = 64
K = 256
NNB = 8
RIM = 32
GROUPS = 4
MEMBERS = 32
DEVICES = GROUPS * MEMBERS
HC = 16
NQ = H // HC
ROWS = 3 * MEMBERS * 2
PAIRS = GROUPS * MEMBERS * 2
EXT = CL + 2 * RIM
BLK = 128
UNROLL = 6
WIN = BLK + 2 * RIM


def dot(a, b):
    return jnp.dot(a, b, preferred_element_type=F32)


def iota(shape, dim):
    return lax.broadcasted_iota(jnp.int32, shape, dim)


def one_hot(mask):
    return jnp.where(mask, 1.0, 0.0).astype(BF16)


def far_offsets():
    dist = (0, 1, 2, 1)
    offsets = [
        (dz, dy, dx, dc) for dz in (2, 1, 3) for dy in range(4) for dx in range(4) for dc in (1, 0)
    ]
    return sorted(offsets, key=lambda o: -(dist[o[0]] + dist[o[1]] + dist[o[2]]))


def kernel(
    src_hbm,
    obs_hbm,
    hist_hbm,
    ntime_hbm,
    nkern_hbm,
    proj_hbm,
    rmap_hbm,
    sinv_hbm,
    inc_hbm,
    nbr_hbm,
    trans_hbm,
    out,
    src,
    obs,
    hv0,
    hv1,
    hv2,
    hv3,
    ntime,
    nkern,
    pv,
    rmap,
    sinv,
    inc,
    nbr,
    trans,
    arows,
    part1,
    perm,
    gone,
    oone,
    sone,
    mone,
    tt,
    rext,
    r1p,
    base,
    outb,
    inb,
    load_sem,
    hist_sem,
    proj_sem,
    send_sem,
    recv_sem,
    halo_send,
    halo_recv,
):
    g = lax.axis_index("group")
    m = lax.axis_index("member")
    me = g * MEMBERS + m
    z, y, x, c = g, m // 8, (m // 2) % 4, m % 2
    right = (m + 1) % MEMBERS
    left = (m + MEMBERS - 1) % MEMBERS

    def peer(o):
        dz, dy, dx, dc = o
        return (z + dz) % 4, ((y + dy) % 4) * 8 + ((x + dx) % 4) * 2 + (c + dc) % 2

    hv = (hv0, hv1, hv2, hv3)

    small = []

    def load(i, a, b):
        cp = pltpu.make_async_copy(a, b, load_sem.at[i])
        cp.start()
        small.append(cp)

    load(0, src_hbm, src)
    load(1, obs_hbm, obs)
    load(2, nbr_hbm, nbr)
    load(3, ntime_hbm, ntime)
    hist_cp = []
    proj_cp = []
    for q in range(NQ):
        cp = pltpu.make_async_copy(hist_hbm.at[:, pl.ds(q * HC, HC)], hv[q], hist_sem.at[q])
        cp.start()
        hist_cp.append(cp)
        cp = pltpu.make_async_copy(
            proj_hbm.at[pl.ds(q * HC * NB, HC * NB)], pv.at[pl.ds(q * HC * NB, HC * NB)], proj_sem.at[q]
        )
        cp.start()
        proj_cp.append(cp)
    load(4, nkern_hbm, nkern)
    load(5, inc_hbm, inc)
    load(6, trans_hbm.at[:, :, pl.ds(0, 128)], trans.at[0])
    load(7, trans_hbm.at[:, :, pl.ds(128, 128)], trans.at[1])
    load(8, rmap_hbm, rmap)
    load(9, sinv_hbm, sinv)

    barrier = pltpu.get_barrier_semaphore()
    for o in far_offsets():
        pl.semaphore_signal(barrier, inc=1, device_id=peer(o), device_id_type=MESH)
    pl.semaphore_signal(barrier, inc=1, device_id=(g, right), device_id_type=MESH)
    pl.semaphore_signal(barrier, inc=1, device_id=(g, left), device_id_type=MESH)

    r = iota((256, 256), 0)
    perm[...] = one_hot(iota((256, 256), 1) == (r % 16) * 16 + r // 16)
    for t in range(2):
        inb[t, :, pl.ds(g * MEMBERS, MEMBERS)] = jnp.zeros((2, MEMBERS, 2, 128), BF16)
    for cp in small[:4]:
        cp.wait()

    tn = ntime[...]
    rr = iota((128, NNB), 0)
    pick = one_hot((rr // 8) % 8 == iota((128, NNB), 1))
    wide = dot(pick, tn).astype(BF16)
    cols = iota((H, 512), 1)
    step = (cols // 128) * 16 + cols % 16
    same = one_hot(iota((H, 512), 0) == step)
    shifted = one_hot(iota((H, 512), 0) == step + 1)
    tr = iota((128, 512), 0)
    tc = iota((128, 512), 1)
    keep = tr % 8 == (tc // 16) % 8
    table = jnp.where(tr < 64, dot(wide, same), dot(wide, shifted))
    tt[...] = jnp.where(keep, table, 0.0).astype(BF16)

    seen = obs[...]
    own = iota((CL, DEVICES), 0)
    by_slot = jnp.concatenate([one_hot(own == seen[s : s + 1]) for s in range(2)], axis=1)
    r = iota((PAIRS, PAIRS), 0)
    weave = one_hot(iota((PAIRS, PAIRS), 1) == (r % DEVICES) * 2 + r // DEVICES)
    oone[...] = dot(by_slot, weave).astype(BF16)
    sub = iota((8, CL), 0)
    lane = iota((8, CL), 1)

    def source_rows(i, carry):
        d = i // 8
        first = ((g + d + 1) % GROUPS) * MEMBERS + (i % 8) * 4
        want = jnp.full((8, CL), -1, jnp.int32)
        for k in range(8):
            want = jnp.where(sub == k, src[k % 2, first + k // 2], want)
        sone[pl.ds(pl.multiple_of(i * 8, 8), 8), :] = jnp.where(lane == want, 1.0, 0.0)
        return carry

    lax.fori_loop(0, ROWS // 8, source_rows, 0)

    wl = iota((BLK, WIN), 1)
    for blk in range(CL // BLK):
        off = me * CL + blk * BLK - RIM
        cols_of = nbr[:, pl.ds(blk * BLK, BLK)].T
        for j in range(NNB):
            col = cols_of[:, j : j + 1] - off
            gone[blk, j] = one_hot(wl == col)

    def gather(q, i):
        d = i // 2
        first = ((g + d + 1) % GROUPS) * MEMBERS + (i % 2) * 16
        parts = [hv[q][jnp.maximum(src[k % 2, first + k // 2], 0)] for k in range(32)]
        tile = jnp.concatenate(
            [jnp.concatenate(parts[:16], axis=0), jnp.concatenate(parts[16:], axis=0)], axis=1
        )
        turned = dot(perm[...], tile).astype(BF16)
        for h in range(HC):
            for s in range(2):
                arows[
                    pl.ds(pl.multiple_of(i * 32 + s * 16, 16), 16), pl.ds((q * HC + h) * NB, NB)
                ] = turned[h * 16 : (h + 1) * 16, s * NB : (s + 1) * NB]

    acc = jnp.zeros((ROWS, K), F32)
    for q in range(NQ):
        hist_cp[q].wait()

        def gathers(i, carry):
            for k in range(UNROLL):
                gather(q, i * UNROLL + k)
            return carry

        lax.fori_loop(0, ROWS // 32 // UNROLL, gathers, 0)
        proj_cp[q].wait()
        acc = acc + dot(
            arows[:, pl.ds(q * HC * NB, HC * NB)], pv[pl.ds(q * HC * NB, HC * NB), :]
        )

    def store_rays(t, rows):
        flat = outb.at[t].reshape(2, ROWS, 128)
        flat[0] = rows[:, :NB]
        flat[1] = rows[:, NB:]

    def send_rays(t):
        for o in far_offsets():
            gg, mm = peer(o)
            pltpu.make_async_remote_copy(
                outb.at[t, :, (o[0] - 1) * MEMBERS + mm],
                inb.at[t, :, me],
                send_sem.at[t],
                recv_sem.at[t],
                device_id=(gg, mm),
                device_id_type=MESH,
            ).start()

    def wait_rays(t):
        part = inb.at[t, :, pl.ds(0, ROWS // 2)]
        pltpu.make_async_copy(part, part, recv_sem.at[t]).wait()

    def halo(t, side):
        if side == 0:
            return pltpu.make_async_remote_copy(
                rext.at[t, :, pl.ds(CL, RIM)],
                rext.at[t, :, pl.ds(0, RIM)],
                halo_send.at[t, 0],
                halo_recv.at[t, 0],
                device_id=(g, right),
                device_id_type=MESH,
            )
        return pltpu.make_async_remote_copy(
            rext.at[t, :, pl.ds(RIM, RIM)],
            rext.at[t, :, pl.ds(RIM + CL, RIM)],
            halo_send.at[t, 1],
            halo_recv.at[t, 1],
            device_id=(g, left),
            device_id_type=MESH,
        )

    outgoing = acc.astype(BF16)
    store_rays(0, outgoing)
    pl.semaphore_wait(barrier, 3 * MEMBERS + 2)
    send_rays(0)

    def reduce_group(i, carry):
        halves = []
        for s in range(2):
            first = pl.multiple_of(i * 16 + s * 8, 8)
            halves.append(
                jnp.concatenate([hv[q][pl.ds(first, 8)].reshape(128, NB) for q in range(NQ)], axis=0)
            )
        red = dot(tt[...], jnp.concatenate(halves, axis=1))
        at = pl.multiple_of(i * 16, 16)
        for j in range(NNB):
            a = red[j * 8 : j * 8 + 8]
            rext[0, j, pl.ds(pl.multiple_of(at + RIM, 16), 16), :] = jnp.concatenate(
                [a[:, :NB], a[:, NB:]], axis=0
            ).astype(BF16)
            b = red[64 + j * 8 : 72 + j * 8]
            r1p[j, pl.ds(at, 16), :] = jnp.concatenate([b[:, :NB], b[:, NB:]], axis=0)
        return carry

    for i in (0, 1, 30, 31):
        reduce_group(i, 0)
    halo(0, 0).start()
    halo(0, 1).start()
    for i in range(2, 30):
        reduce_group(i, 0)

    part1[...] = dot(arows[:, : (H - 1) * NB], pv[NB:, :])
    mone[...] = dot(sone[...].astype(BF16), oone[...]).astype(BF16)

    for cp in small[4:]:
        cp.wait()

    def near_block(t, blk):
        picked = [
            dot(gone[blk, j], rext[t, j, pl.ds(blk * BLK, WIN), :]).astype(BF16) for j in range(NNB)
        ]
        near = dot(jnp.concatenate(picked, axis=1), nkern[...])
        base[pl.ds(blk * BLK, BLK), :] = inc[t, pl.ds(blk * BLK, BLK), :] - near

    def near_field(t):
        near_block(t, 1)
        near_block(t, 2)
        halo(t, 0).wait_recv()
        near_block(t, 0)
        halo(t, 1).wait_recv()
        near_block(t, 3)

    def contributions(t):
        rays = inb.at[t].reshape(2, PAIRS, 128)
        factor = trans.reshape(2, PAIRS, 128)
        halves = [factor[s].astype(F32) * rays[s].astype(F32) for s in range(2)]
        full = jnp.concatenate(halves, axis=1)
        high = full.astype(BF16)
        low = (full - high.astype(F32)).astype(BF16)
        return high, low

    near_field(0)
    full = base[...]
    b0 = full.astype(BF16)
    rest = full - b0.astype(F32)
    b1 = rest.astype(BF16)
    b2 = (rest - b1.astype(F32)).astype(BF16)
    sel = sone[...].astype(BF16)
    base_src = dot(sel, b0) + dot(sel, b1) + dot(sel, b2)

    wait_rays(0)
    high, low = contributions(0)

    def currents(hot, start):
        incoming = (dot(hot, high) + dot(hot, low)).astype(BF16)
        rhs = (start - dot(incoming, rmap[...])).astype(BF16)
        return dot(rhs, sinv[...])

    at_src = currents(mone[...], base_src).astype(BF16)
    outgoing = (part1[...] + dot(at_src, pv[:NB, :])).astype(BF16)
    store_rays(1, outgoing)
    send_rays(1)

    cur0 = currents(oone[...], base[...])
    out[0] = cur0
    newest = cur0.astype(BF16).astype(F32)
    for j in range(NNB):
        weight = ntime[j : j + 1, 0:1].astype(F32)
        rext[1, j, pl.ds(RIM, CL), :] = (r1p[j] + weight * newest).astype(BF16)
    halo(1, 0).start()
    halo(1, 1).start()
    near_field(1)

    wait_rays(1)
    high, low = contributions(1)
    out[1] = currents(oone[...], base[...])
    for t in range(2):
        halo(t, 0).wait_send()
        halo(t, 1).wait_send()
        pltpu.make_async_copy(outb.at[t], outb.at[t], send_sem.at[t]).wait()


def body(
    history,
    near_time,
    near_kernel,
    projection,
    receive_map,
    self_inverse,
    incident,
    neighbours,
    send_sources,
    recv_observers,
    transfer,
):
    args = (
        send_sources.reshape(DEVICES, 2).T,
        recv_observers.reshape(DEVICES, 2).T,
        history,
        near_time,
        near_kernel.reshape(NNB * NB, NB),
        projection.reshape(H * NB, K),
        receive_map,
        self_inverse,
        incident,
        neighbours.T,
        transfer.reshape(DEVICES, 2, K),
    )
    scratch = [
        pltpu.SMEM((2, DEVICES), jnp.int32),
        pltpu.VMEM((2, DEVICES), jnp.int32),
        *[pltpu.VMEM((CL, HC, NB), BF16) for _ in range(NQ)],
        pltpu.VMEM((NNB, H), BF16),
        pltpu.VMEM((NNB * NB, NB), BF16),
        pltpu.VMEM((H * NB, K), BF16),
        pltpu.VMEM((K, NB), BF16),
        pltpu.VMEM((NB, NB), BF16),
        pltpu.VMEM((2, CL, NB), F32),
        pltpu.VMEM((NNB, CL), jnp.int32),
        pltpu.VMEM((2, DEVICES, 2, 128), BF16),
        pltpu.VMEM((ROWS, H * NB), BF16),
        pltpu.VMEM((ROWS, K), F32),
        pltpu.VMEM((256, 256), BF16),
        pltpu.VMEM((CL // BLK, NNB, BLK, WIN), BF16),
        pltpu.VMEM((CL, PAIRS), BF16),
        pltpu.VMEM((ROWS, CL), F32),
        pltpu.VMEM((ROWS, PAIRS), BF16),
        pltpu.VMEM((128, 512), BF16),
        pltpu.VMEM((2, NNB, EXT, NB), BF16),
        pltpu.VMEM((NNB, CL, NB), F32),
        pltpu.VMEM((CL, NB), F32),
        pltpu.VMEM((2, 2, ROWS // 2, 2, 128), BF16),
        pltpu.VMEM((2, 2, PAIRS // 2, 2, 128), BF16),
        pltpu.SemaphoreType.DMA((10,)),
        pltpu.SemaphoreType.DMA((NQ,)),
        pltpu.SemaphoreType.DMA((NQ,)),
        pltpu.SemaphoreType.DMA((2,)),
        pltpu.SemaphoreType.DMA((2,)),
        pltpu.SemaphoreType.DMA((2, 2)),
        pltpu.SemaphoreType.DMA((2, 2)),
    ]
    return pl.pallas_call(
        kernel,
        out_shape=jax.ShapeDtypeStruct((2, CL, NB), F32),
        in_specs=[pl.BlockSpec(memory_space=pltpu.HBM)] * len(args),
        out_specs=pl.BlockSpec(memory_space=pltpu.VMEM),
        scratch_shapes=scratch,
        compiler_params=pltpu.CompilerParams(
            collective_id=0, has_side_effects=True, vmem_limit_bytes=64 << 20
        ),
        cost_estimate=pl.CostEstimate(
            flops=4_000_000_000, bytes_accessed=14 << 20, transcendentals=0
        ),
    )(*args)


def solution(mesh):
    both = ("group", "member")
    in_specs = (
        P(both, None, None),
        P(),
        P(),
        P(),
        P(),
        P(),
        P(None, both, None),
        P(both, None),
        P(both, None, None),
        P(both, None, None),
        P(both, None, None, None),
    )
    out_specs = P(None, both, None)
    return jax.shard_map(body, mesh=mesh, in_specs=in_specs, out_specs=out_specs, check_vma=False)
```

```python
import functools

import jax
import jax.numpy as jnp
from jax import lax
from jax.experimental import pallas as pl
from jax.experimental.pallas import tpu as pltpu
from jax.sharding import PartitionSpec as P

MESH = pl.DeviceIdType.MESH
BF16 = jnp.bfloat16
F32 = jnp.float32

CL = 512
NB = 128
H = 64
K = 256
NNB = 8
RIM = 32
GROUPS = 4
MEMBERS = 32
DEVICES = GROUPS * MEMBERS
HC = 16
NQ = H // HC
ROWS = 3 * MEMBERS * 2
PAIRS = GROUPS * MEMBERS * 2
EXT = CL + 2 * RIM
BLK = 128
UNROLL = 6
WIN = BLK + 2 * RIM


def dot(a, b):
    return jnp.dot(a, b, preferred_element_type=F32)


def iota(shape, dim):
    return lax.broadcasted_iota(jnp.int32, shape, dim)


def one_hot(mask):
    return jnp.where(mask, 1.0, 0.0).astype(BF16)


def far_offsets():
    dist = (0, 1, 2, 1)
    offsets = [
        (dz, dy, dx, dc) for dz in (2, 1, 3) for dy in range(4) for dx in range(4) for dc in (1, 0)
    ]
    return sorted(offsets, key=lambda o: -(dist[o[0]] + dist[o[1]] + dist[o[2]]))


def kernel(
    src_hbm,
    obs_hbm,
    hist_hbm,
    ntime_hbm,
    nkern_hbm,
    proj_hbm,
    rmap_hbm,
    sinv_hbm,
    inc_hbm,
    nbr_hbm,
    trans_hbm,
    out,
    src,
    obs,
    hv0,
    hv1,
    hv2,
    hv3,
    ntime,
    nkern,
    pv,
    rmap,
    sinv,
    inc,
    nbr,
    trans,
    arows,
    part1,
    perm,
    gone,
    oone,
    sone,
    mone,
    tt,
    rext,
    r1p,
    base,
    outb,
    inb,
    load_sem,
    hist_sem,
    proj_sem,
    send_sem,
    recv_sem,
    halo_send,
    halo_recv,
):
    g = lax.axis_index("group")
    m = lax.axis_index("member")
    me = g * MEMBERS + m
    z, y, x, c = g, m // 8, (m // 2) % 4, m % 2
    right = (m + 1) % MEMBERS
    left = (m + MEMBERS - 1) % MEMBERS

    def peer(o):
        dz, dy, dx, dc = o
        return (z + dz) % 4, ((y + dy) % 4) * 8 + ((x + dx) % 4) * 2 + (c + dc) % 2

    hv = (hv0, hv1, hv2, hv3)

    small = []

    def load(i, a, b):
        cp = pltpu.make_async_copy(a, b, load_sem.at[i])
        cp.start()
        small.append(cp)

    load(0, src_hbm, src)
    load(1, obs_hbm, obs)
    load(2, nbr_hbm, nbr)
    load(3, ntime_hbm, ntime)
    hist_cp = []
    proj_cp = []
    for q in range(NQ):
        cp = pltpu.make_async_copy(hist_hbm.at[:, pl.ds(q * HC, HC)], hv[q], hist_sem.at[q])
        cp.start()
        hist_cp.append(cp)
        cp = pltpu.make_async_copy(
            proj_hbm.at[pl.ds(q * HC * NB, HC * NB)], pv.at[pl.ds(q * HC * NB, HC * NB)], proj_sem.at[q]
        )
        cp.start()
        proj_cp.append(cp)
    load(4, nkern_hbm, nkern)
    load(5, inc_hbm, inc)
    load(6, trans_hbm.at[:, :, pl.ds(0, 128)], trans.at[0])
    load(7, trans_hbm.at[:, :, pl.ds(128, 128)], trans.at[1])
    load(8, rmap_hbm, rmap)
    load(9, sinv_hbm, sinv)

    barrier = pltpu.get_barrier_semaphore()
    for o in far_offsets():
        pl.semaphore_signal(barrier, inc=1, device_id=peer(o), device_id_type=MESH)
    pl.semaphore_signal(barrier, inc=1, device_id=(g, right), device_id_type=MESH)
    pl.semaphore_signal(barrier, inc=1, device_id=(g, left), device_id_type=MESH)

    r = iota((256, 256), 0)
    perm[...] = one_hot(iota((256, 256), 1) == (r % 16) * 16 + r // 16)
    for t in range(2):
        inb[t, :, pl.ds(g * MEMBERS, MEMBERS)] = jnp.zeros((2, MEMBERS, 2, 128), BF16)
    for cp in small[:4]:
        cp.wait()

    tn = ntime[...]
    rr = iota((128, NNB), 0)
    pick = one_hot((rr // 8) % 8 == iota((128, NNB), 1))
    wide = dot(pick, tn).astype(BF16)
    cols = iota((H, 512), 1)
    step = (cols // 128) * 16 + cols % 16
    same = one_hot(iota((H, 512), 0) == step)
    shifted = one_hot(iota((H, 512), 0) == step + 1)
    tr = iota((128, 512), 0)
    tc = iota((128, 512), 1)
    keep = tr % 8 == (tc // 16) % 8
    table = jnp.where(tr < 64, dot(wide, same), dot(wide, shifted))
    tt[...] = jnp.where(keep, table, 0.0).astype(BF16)

    seen = obs[...]
    own = iota((CL, DEVICES), 0)
    by_slot = jnp.concatenate([one_hot(own == seen[s : s + 1]) for s in range(2)], axis=1)
    r = iota((PAIRS, PAIRS), 0)
    weave = one_hot(iota((PAIRS, PAIRS), 1) == (r % DEVICES) * 2 + r // DEVICES)
    oone[...] = dot(by_slot, weave).astype(BF16)
    sub = iota((8, CL), 0)
    lane = iota((8, CL), 1)

    def source_rows(i, carry):
        d = i // 8
        first = ((g + d + 1) % GROUPS) * MEMBERS + (i % 8) * 4
        want = jnp.full((8, CL), -1, jnp.int32)
        for k in range(8):
            want = jnp.where(sub == k, src[k % 2, first + k // 2], want)
        sone[pl.ds(pl.multiple_of(i * 8, 8), 8), :] = jnp.where(lane == want, 1.0, 0.0)
        return carry

    lax.fori_loop(0, ROWS // 8, source_rows, 0)

    wl = iota((BLK, WIN), 1)
    for blk in range(CL // BLK):
        off = me * CL + blk * BLK - RIM
        cols_of = nbr[:, pl.ds(blk * BLK, BLK)].T
        for j in range(NNB):
            col = cols_of[:, j : j + 1] - off
            gone[blk, j] = one_hot(wl == col)

    def gather(q, i):
        d = i // 2
        first = ((g + d + 1) % GROUPS) * MEMBERS + (i % 2) * 16
        parts = [hv[q][jnp.maximum(src[k % 2, first + k // 2], 0)] for k in range(32)]
        tile = jnp.concatenate(
            [jnp.concatenate(parts[:16], axis=0), jnp.concatenate(parts[16:], axis=0)], axis=1
        )
        turned = dot(perm[...], tile).astype(BF16)
        for h in range(HC):
            for s in range(2):
                arows[
                    pl.ds(pl.multiple_of(i * 32 + s * 16, 16), 16), pl.ds((q * HC + h) * NB, NB)
                ] = turned[h * 16 : (h + 1) * 16, s * NB : (s + 1) * NB]

    acc = jnp.zeros((ROWS, K), F32)
    for q in range(NQ):
        hist_cp[q].wait()

        def gathers(i, carry):
            for k in range(UNROLL):
                gather(q, i * UNROLL + k)
            return carry

        lax.fori_loop(0, ROWS // 32 // UNROLL, gathers, 0)
        proj_cp[q].wait()
        acc = acc + dot(
            arows[:, pl.ds(q * HC * NB, HC * NB)], pv[pl.ds(q * HC * NB, HC * NB), :]
        )

    def store_rays(t, rows):
        flat = outb.at[t].reshape(2, ROWS, 128)
        flat[0] = rows[:, :NB]
        flat[1] = rows[:, NB:]

    def send_rays(t):
        for o in far_offsets():
            gg, mm = peer(o)
            pltpu.make_async_remote_copy(
                outb.at[t, :, (o[0] - 1) * MEMBERS + mm],
                inb.at[t, :, me],
                send_sem.at[t],
                recv_sem.at[t],
                device_id=(gg, mm),
                device_id_type=MESH,
            ).start()

    def wait_rays(t):
        part = inb.at[t, :, pl.ds(0, ROWS // 2)]
        pltpu.make_async_copy(part, part, recv_sem.at[t]).wait()

    def halo(t, side):
        if side == 0:
            return pltpu.make_async_remote_copy(
                rext.at[t, :, pl.ds(CL, RIM)],
                rext.at[t, :, pl.ds(0, RIM)],
                halo_send.at[t, 0],
                halo_recv.at[t, 0],
                device_id=(g, right),
                device_id_type=MESH,
            )
        return pltpu.make_async_remote_copy(
            rext.at[t, :, pl.ds(RIM, RIM)],
            rext.at[t, :, pl.ds(RIM + CL, RIM)],
            halo_send.at[t, 1],
            halo_recv.at[t, 1],
            device_id=(g, left),
            device_id_type=MESH,
        )

    outgoing = acc.astype(BF16)
    store_rays(0, outgoing)
    pl.semaphore_wait(barrier, 3 * MEMBERS + 2)
    send_rays(0)

    def reduce_group(i, carry):
        halves = []
        for s in range(2):
            first = pl.multiple_of(i * 16 + s * 8, 8)
            halves.append(
                jnp.concatenate([hv[q][pl.ds(first, 8)].reshape(128, NB) for q in range(NQ)], axis=0)
            )
        red = dot(tt[...], jnp.concatenate(halves, axis=1))
        at = pl.multiple_of(i * 16, 16)
        for j in range(NNB):
            a = red[j * 8 : j * 8 + 8]
            rext[0, j, pl.ds(pl.multiple_of(at + RIM, 16), 16), :] = jnp.concatenate(
                [a[:, :NB], a[:, NB:]], axis=0
            ).astype(BF16)
            b = red[64 + j * 8 : 72 + j * 8]
            r1p[j, pl.ds(at, 16), :] = jnp.concatenate([b[:, :NB], b[:, NB:]], axis=0)
        return carry

    for i in (0, 1, 30, 31):
        reduce_group(i, 0)
    halo(0, 0).start()
    halo(0, 1).start()
    for i in range(2, 30):
        reduce_group(i, 0)

    part1[...] = dot(arows[:, : (H - 1) * NB], pv[NB:, :])
    mone[...] = dot(sone[...].astype(BF16), oone[...]).astype(BF16)

    for cp in small[4:]:
        cp.wait()

    def near_block(t, blk):
        picked = [
            dot(gone[blk, j], rext[t, j, pl.ds(blk * BLK, WIN), :]).astype(BF16) for j in range(NNB)
        ]
        near = dot(jnp.concatenate(picked, axis=1), nkern[...])
        base[pl.ds(blk * BLK, BLK), :] = inc[t, pl.ds(blk * BLK, BLK), :] - near

    def near_field(t):
        near_block(t, 1)
        near_block(t, 2)
        halo(t, 0).wait_recv()
        near_block(t, 0)
        halo(t, 1).wait_recv()
        near_block(t, 3)

    def contributions(t):
        rays = inb.at[t].reshape(2, PAIRS, 128)
        factor = trans.reshape(2, PAIRS, 128)
        halves = [factor[s].astype(F32) * rays[s].astype(F32) for s in range(2)]
        full = jnp.concatenate(halves, axis=1)
        high = full.astype(BF16)
        low = (full - high.astype(F32)).astype(BF16)
        return high, low

    near_field(0)
    full = base[...]
    b0 = full.astype(BF16)
    rest = full - b0.astype(F32)
    b1 = rest.astype(BF16)
    b2 = (rest - b1.astype(F32)).astype(BF16)
    sel = sone[...].astype(BF16)
    base_src = dot(sel, b0) + dot(sel, b1) + dot(sel, b2)

    wait_rays(0)
    high, low = contributions(0)

    def currents(hot, start):
        incoming = (dot(hot, high) + dot(hot, low)).astype(BF16)
        rhs = (start - dot(incoming, rmap[...])).astype(BF16)
        return dot(rhs, sinv[...])

    at_src = currents(mone[...], base_src).astype(BF16)
    outgoing = (part1[...] + dot(at_src, pv[:NB, :])).astype(BF16)
    store_rays(1, outgoing)
    send_rays(1)

    cur0 = currents(oone[...], base[...])
    out[0] = cur0
    newest = cur0.astype(BF16).astype(F32)
    for j in range(NNB):
        weight = ntime[j : j + 1, 0:1].astype(F32)
        rext[1, j, pl.ds(RIM, CL), :] = (r1p[j] + weight * newest).astype(BF16)
    halo(1, 0).start()
    halo(1, 1).start()
    near_field(1)

    wait_rays(1)
    high, low = contributions(1)
    out[1] = currents(oone[...], base[...])
    for t in range(2):
        halo(t, 0).wait_send()
        halo(t, 1).wait_send()
        pltpu.make_async_copy(outb.at[t], outb.at[t], send_sem.at[t]).wait()


def body(
    history,
    near_time,
    near_kernel,
    projection,
    receive_map,
    self_inverse,
    incident,
    neighbours,
    send_sources,
    recv_observers,
    transfer,
):
    args = (
        send_sources.reshape(DEVICES, 2).T,
        recv_observers.reshape(DEVICES, 2).T,
        history,
        near_time,
        near_kernel.reshape(NNB * NB, NB),
        projection.reshape(H * NB, K),
        receive_map,
        self_inverse,
        incident,
        neighbours.T,
        transfer.reshape(DEVICES, 2, K),
    )
    scratch = [
        pltpu.SMEM((2, DEVICES), jnp.int32),
        pltpu.VMEM((2, DEVICES), jnp.int32),
        *[pltpu.VMEM((CL, HC, NB), BF16) for _ in range(NQ)],
        pltpu.VMEM((NNB, H), BF16),
        pltpu.VMEM((NNB * NB, NB), BF16),
        pltpu.VMEM((H * NB, K), BF16),
        pltpu.VMEM((K, NB), BF16),
        pltpu.VMEM((NB, NB), BF16),
        pltpu.VMEM((2, CL, NB), F32),
        pltpu.VMEM((NNB, CL), jnp.int32),
        pltpu.VMEM((2, DEVICES, 2, 128), BF16),
        pltpu.VMEM((ROWS, H * NB), BF16),
        pltpu.VMEM((ROWS, K), F32),
        pltpu.VMEM((256, 256), BF16),
        pltpu.VMEM((CL // BLK, NNB, BLK, WIN), BF16),
        pltpu.VMEM((CL, PAIRS), BF16),
        pltpu.VMEM((ROWS, CL), F32),
        pltpu.VMEM((ROWS, PAIRS), BF16),
        pltpu.VMEM((128, 512), BF16),
        pltpu.VMEM((2, NNB, EXT, NB), BF16),
        pltpu.VMEM((NNB, CL, NB), F32),
        pltpu.VMEM((CL, NB), F32),
        pltpu.VMEM((2, 2, ROWS // 2, 2, 128), BF16),
        pltpu.VMEM((2, 2, PAIRS // 2, 2, 128), BF16),
        pltpu.SemaphoreType.DMA((10,)),
        pltpu.SemaphoreType.DMA((NQ,)),
        pltpu.SemaphoreType.DMA((NQ,)),
        pltpu.SemaphoreType.DMA((2,)),
        pltpu.SemaphoreType.DMA((2,)),
        pltpu.SemaphoreType.DMA((2, 2)),
        pltpu.SemaphoreType.DMA((2, 2)),
    ]
    return pl.pallas_call(
        kernel,
        out_shape=pltpu.VMEM((2, CL, NB), F32),
        in_specs=[pl.BlockSpec(memory_space=pltpu.HBM)] * len(args),
        out_specs=pl.BlockSpec(memory_space=pltpu.VMEM),
        scratch_shapes=scratch,
        compiler_params=pltpu.CompilerParams(
            collective_id=0, has_side_effects=True, vmem_limit_bytes=48 << 20
        ),
        cost_estimate=pl.CostEstimate(
            flops=4_000_000_000, bytes_accessed=14 << 20, transcendentals=0
        ),
    )(*[pltpu.with_memory_space_constraint(a, pltpu.HBM) for a in args])


def solution(mesh):
    both = ("group", "member")
    in_specs = (
        P(both, None, None),
        P(),
        P(),
        P(),
        P(),
        P(),
        P(None, both, None),
        P(both, None),
        P(both, None, None),
        P(both, None, None),
        P(both, None, None, None),
    )
    out_specs = P(None, both, None)
    return jax.shard_map(body, mesh=mesh, in_specs=in_specs, out_specs=out_specs, check_vma=False)
```

```python
import functools

import jax
import jax.numpy as jnp
from jax import lax
from jax.experimental import pallas as pl
from jax.experimental.pallas import tpu as pltpu
from jax.sharding import PartitionSpec as P

MESH = pl.DeviceIdType.MESH
BF16 = jnp.bfloat16
F32 = jnp.float32

CL = 512
NB = 128
H = 64
K = 256
NNB = 8
RIM = 32
GROUPS = 4
MEMBERS = 32
DEVICES = GROUPS * MEMBERS
HC = 16
NQ = H // HC
ROWS = 3 * MEMBERS * 2
PAIRS = GROUPS * MEMBERS * 2
EXT = CL + 2 * RIM
BLK = 128
UNROLL = 6
WIN = BLK + 2 * RIM


def dot(a, b):
    return jnp.dot(a, b, preferred_element_type=F32)


def iota(shape, dim):
    return lax.broadcasted_iota(jnp.int32, shape, dim)


def one_hot(mask):
    return jnp.where(mask, 1.0, 0.0).astype(BF16)


def far_offsets():
    dist = (0, 1, 2, 1)
    offsets = [
        (dz, dy, dx, dc) for dz in (2, 1, 3) for dy in range(4) for dx in range(4) for dc in (1, 0)
    ]
    return sorted(offsets, key=lambda o: -(dist[o[0]] + dist[o[1]] + dist[o[2]]))


def kernel(
    src_hbm,
    obs_hbm,
    hist_hbm,
    ntime_hbm,
    nkern_hbm,
    proj_hbm,
    rmap_hbm,
    sinv_hbm,
    inc_hbm,
    nbr_hbm,
    trans_hbm,
    out,
    src,
    obs,
    hv0,
    hv1,
    hv2,
    hv3,
    ntime,
    nkern,
    pv,
    rmap,
    sinv,
    inc,
    nbr,
    trans,
    arows,
    part1,
    perm,
    gone,
    oone,
    sone,
    mone,
    tt,
    rext,
    r1p,
    base,
    outb,
    inb,
    load_sem,
    hist_sem,
    proj_sem,
    send_sem,
    recv_sem,
    halo_send,
    halo_recv,
):
    g = lax.axis_index("group")
    m = lax.axis_index("member")
    me = g * MEMBERS + m
    y, x, c = lax.div(m, 8), lax.rem(lax.div(m, 2), 4), lax.rem(m, 2)
    at_z = [lax.rem(g + d, 4) for d in range(4)]
    at_y = [lax.rem(y + d, 4) * 8 for d in range(4)]
    at_x = [lax.rem(x + d, 4) * 2 for d in range(4)]
    at_c = [c, 1 - c]
    at_yx = [[a + b for b in at_x] for a in at_y]
    at_member = [[[a + b for b in at_c] for a in row] for row in at_yx]
    right = (m + 1) % MEMBERS
    left = (m + MEMBERS - 1) % MEMBERS

    def peer(o):
        dz, dy, dx, dc = o
        return at_z[dz], at_member[dy][dx][dc]

    hv = (hv0, hv1, hv2, hv3)

    small = []

    def load(i, a, b):
        cp = pltpu.make_async_copy(a, b, load_sem.at[i])
        cp.start()
        small.append(cp)

    load(0, src_hbm, src)
    load(1, obs_hbm, obs)
    load(2, nbr_hbm, nbr)
    load(3, ntime_hbm, ntime)
    hist_cp = []
    proj_cp = []
    for q in range(NQ):
        cp = pltpu.make_async_copy(hist_hbm.at[:, pl.ds(q * HC, HC)], hv[q], hist_sem.at[q])
        cp.start()
        hist_cp.append(cp)
        cp = pltpu.make_async_copy(
            proj_hbm.at[pl.ds(q * HC * NB, HC * NB)], pv.at[pl.ds(q * HC * NB, HC * NB)], proj_sem.at[q]
        )
        cp.start()
        proj_cp.append(cp)
    load(4, nkern_hbm, nkern)
    load(5, inc_hbm, inc)
    load(6, trans_hbm.at[:, :, pl.ds(0, 128)], trans.at[0])
    load(7, trans_hbm.at[:, :, pl.ds(128, 128)], trans.at[1])
    load(8, rmap_hbm, rmap)
    load(9, sinv_hbm, sinv)

    barrier = pltpu.get_barrier_semaphore()
    for o in far_offsets():
        pl.semaphore_signal(barrier, inc=1, device_id=peer(o), device_id_type=MESH)
    pl.semaphore_signal(barrier, inc=1, device_id=(g, right), device_id_type=MESH)
    pl.semaphore_signal(barrier, inc=1, device_id=(g, left), device_id_type=MESH)

    r = iota((256, 256), 0)
    perm[...] = one_hot(iota((256, 256), 1) == (r % 16) * 16 + r // 16)
    for t in range(2):
        inb[t, :, pl.ds(g * MEMBERS, MEMBERS)] = jnp.zeros((2, MEMBERS, 2, 128), BF16)
    for cp in small[:4]:
        cp.wait()

    tn = ntime[...]
    rr = iota((128, NNB), 0)
    pick = one_hot((rr // 8) % 8 == iota((128, NNB), 1))
    wide = dot(pick, tn).astype(BF16)
    cols = iota((H, 512), 1)
    step = (cols // 128) * 16 + cols % 16
    same = one_hot(iota((H, 512), 0) == step)
    shifted = one_hot(iota((H, 512), 0) == step + 1)
    tr = iota((128, 512), 0)
    tc = iota((128, 512), 1)
    keep = tr % 8 == (tc // 16) % 8
    table = jnp.where(tr < 64, dot(wide, same), dot(wide, shifted))
    tt[...] = jnp.where(keep, table, 0.0).astype(BF16)

    seen = obs[...]
    own = iota((CL, DEVICES), 0)
    by_slot = jnp.concatenate([one_hot(own == seen[s : s + 1]) for s in range(2)], axis=1)
    r = iota((PAIRS, PAIRS), 0)
    weave = one_hot(iota((PAIRS, PAIRS), 1) == (r % DEVICES) * 2 + r // DEVICES)
    woven = dot(by_slot, weave).astype(BF16)
    oone[...] = jnp.concatenate([woven, woven], axis=1)
    sub = iota((8, CL), 0)
    lane = iota((8, CL), 1)

    def source_rows(i, carry):
        d = i // 8
        first = ((g + d + 1) % GROUPS) * MEMBERS + (i % 8) * 4
        want = jnp.full((8, CL), -1, jnp.int32)
        for k in range(8):
            want = jnp.where(sub == k, src[k % 2, first + k // 2], want)
        sone[pl.ds(pl.multiple_of(i * 8, 8), 8), :] = jnp.where(lane == want, 1.0, 0.0)
        return carry

    lax.fori_loop(0, ROWS // 8, source_rows, 0)

    wl = iota((BLK, WIN), 1)
    for blk in range(CL // BLK):
        off = me * CL + blk * BLK - RIM
        cols_of = nbr[:, pl.ds(blk * BLK, BLK)].T
        for j in range(NNB):
            col = cols_of[:, j : j + 1] - off
            gone[blk, j] = one_hot(wl == col)

    def gather(q, i):
        d = i // 2
        first = ((g + d + 1) % GROUPS) * MEMBERS + (i % 2) * 16
        parts = [hv[q][jnp.maximum(src[k % 2, first + k // 2], 0)] for k in range(32)]
        tile = jnp.concatenate(
            [jnp.concatenate(parts[:16], axis=0), jnp.concatenate(parts[16:], axis=0)], axis=1
        )
        turned = dot(perm[...], tile).astype(BF16)
        for h in range(HC):
            for s in range(2):
                arows[
                    pl.ds(pl.multiple_of(i * 32 + s * 16, 16), 16), pl.ds((q * HC + h) * NB, NB)
                ] = turned[h * 16 : (h + 1) * 16, s * NB : (s + 1) * NB]

    acc = jnp.zeros((ROWS, K), F32)
    for q in range(NQ):
        hist_cp[q].wait()

        def gathers(i, carry):
            for k in range(UNROLL):
                gather(q, i * UNROLL + k)
            return carry

        lax.fori_loop(0, ROWS // 32 // UNROLL, gathers, 0)
        proj_cp[q].wait()
        acc = acc + dot(
            arows[:, pl.ds(q * HC * NB, HC * NB)], pv[pl.ds(q * HC * NB, HC * NB), :]
        )

    def store_rays(t, rows):
        flat = outb.at[t].reshape(2, ROWS, 128)
        flat[0] = rows[:, :NB]
        flat[1] = rows[:, NB:]

    def send_rays(t):
        for o in far_offsets():
            gg, mm = peer(o)
            pltpu.make_async_remote_copy(
                outb.at[t, :, (o[0] - 1) * MEMBERS + mm],
                inb.at[t, :, me],
                send_sem.at[t],
                recv_sem.at[t],
                device_id=(gg, mm),
                device_id_type=MESH,
            ).start()

    def wait_rays(t):
        part = inb.at[t, :, pl.ds(0, ROWS // 2)]
        pltpu.make_async_copy(part, part, recv_sem.at[t]).wait()

    def halo(t, side):
        if side == 0:
            return pltpu.make_async_remote_copy(
                rext.at[t, :, pl.ds(CL, RIM)],
                rext.at[t, :, pl.ds(0, RIM)],
                halo_send.at[t, 0],
                halo_recv.at[t, 0],
                device_id=(g, right),
                device_id_type=MESH,
            )
        return pltpu.make_async_remote_copy(
            rext.at[t, :, pl.ds(RIM, RIM)],
            rext.at[t, :, pl.ds(RIM + CL, RIM)],
            halo_send.at[t, 1],
            halo_recv.at[t, 1],
            device_id=(g, left),
            device_id_type=MESH,
        )

    outgoing = acc.astype(BF16)
    store_rays(0, outgoing)
    pl.semaphore_wait(barrier, 3 * MEMBERS + 2)
    send_rays(0)

    def reduce_group(i, carry):
        halves = []
        for s in range(2):
            first = pl.multiple_of(i * 16 + s * 8, 8)
            halves.append(
                jnp.concatenate([hv[q][pl.ds(first, 8)].reshape(128, NB) for q in range(NQ)], axis=0)
            )
        red = dot(tt[...], jnp.concatenate(halves, axis=1))
        at = pl.multiple_of(i * 16, 16)
        for j in range(NNB):
            a = red[j * 8 : j * 8 + 8]
            rext[0, j, pl.ds(pl.multiple_of(at + RIM, 16), 16), :] = jnp.concatenate(
                [a[:, :NB], a[:, NB:]], axis=0
            ).astype(BF16)
            b = red[64 + j * 8 : 72 + j * 8]
            r1p[j, pl.ds(at, 16), :] = jnp.concatenate([b[:, :NB], b[:, NB:]], axis=0)
        return carry

    for i in (0, 1, 30, 31):
        reduce_group(i, 0)
    halo(0, 0).start()
    halo(0, 1).start()
    for i in range(2, 30):
        reduce_group(i, 0)

    part1[...] = dot(arows[:, : (H - 1) * NB], pv[NB:, :])
    mone[...] = dot(sone[...].astype(BF16), oone[...]).astype(BF16)

    for cp in small[4:]:
        cp.wait()

    def near_block(t, blk):
        picked = [
            dot(gone[blk, j], rext[t, j, pl.ds(blk * BLK, WIN), :]).astype(BF16) for j in range(NNB)
        ]
        near = dot(jnp.concatenate(picked, axis=1), nkern[...])
        base[pl.ds(blk * BLK, BLK), :] = inc[t, pl.ds(blk * BLK, BLK), :] - near

    def near_field(t):
        near_block(t, 1)
        near_block(t, 2)
        halo(t, 0).wait_recv()
        near_block(t, 0)
        halo(t, 1).wait_recv()
        near_block(t, 3)

    def contributions(t):
        rays = inb.at[t].reshape(2, PAIRS, 128)
        factor = trans.reshape(2, PAIRS, 128)
        halves = [factor[s].astype(F32) * rays[s].astype(F32) for s in range(2)]
        full = jnp.concatenate(halves, axis=1)
        high = full.astype(BF16)
        low = (full - high.astype(F32)).astype(BF16)
        return jnp.concatenate([high, low], axis=0)

    near_field(0)
    full = base[...]
    b0 = full.astype(BF16)
    rest = full - b0.astype(F32)
    b1 = rest.astype(BF16)
    b2 = (rest - b1.astype(F32)).astype(BF16)
    sel = sone[...].astype(BF16)
    parts = dot(sel, jnp.concatenate([b0, b1, b2], axis=1))
    base_src = parts[:, :NB] + parts[:, NB : 2 * NB] + parts[:, 2 * NB :]

    wait_rays(0)
    terms = contributions(0)

    def currents(hot, start):
        incoming = dot(hot, terms).astype(BF16)
        rhs = (start - dot(incoming, rmap[...])).astype(BF16)
        return dot(rhs, sinv[...])

    at_src = currents(mone[...], base_src).astype(BF16)
    outgoing = (part1[...] + dot(at_src, pv[:NB, :])).astype(BF16)
    store_rays(1, outgoing)
    send_rays(1)

    cur0 = currents(oone[...], base[...])
    out[0] = cur0
    newest = cur0.astype(BF16).astype(F32)
    for j in range(NNB):
        weight = ntime[j : j + 1, 0:1].astype(F32)
        rext[1, j, pl.ds(RIM, CL), :] = (r1p[j] + weight * newest).astype(BF16)
    halo(1, 0).start()
    halo(1, 1).start()
    near_field(1)

    wait_rays(1)
    terms = contributions(1)
    out[1] = currents(oone[...], base[...])
    for t in range(2):
        halo(t, 0).wait_send()
        halo(t, 1).wait_send()
        pltpu.make_async_copy(outb.at[t], outb.at[t], send_sem.at[t]).wait()


def body(
    history,
    near_time,
    near_kernel,
    projection,
    receive_map,
    self_inverse,
    incident,
    neighbours,
    send_sources,
    recv_observers,
    transfer,
):
    args = (
        send_sources.reshape(DEVICES, 2).T,
        recv_observers.reshape(DEVICES, 2).T,
        history,
        near_time,
        near_kernel.reshape(NNB * NB, NB),
        projection.reshape(H * NB, K),
        receive_map,
        self_inverse,
        incident,
        neighbours.T,
        transfer.reshape(DEVICES, 2, K),
    )
    scratch = [
        pltpu.SMEM((2, DEVICES), jnp.int32),
        pltpu.VMEM((2, DEVICES), jnp.int32),
        *[pltpu.VMEM((CL, HC, NB), BF16) for _ in range(NQ)],
        pltpu.VMEM((NNB, H), BF16),
        pltpu.VMEM((NNB * NB, NB), BF16),
        pltpu.VMEM((H * NB, K), BF16),
        pltpu.VMEM((K, NB), BF16),
        pltpu.VMEM((NB, NB), BF16),
        pltpu.VMEM((2, CL, NB), F32),
        pltpu.VMEM((NNB, CL), jnp.int32),
        pltpu.VMEM((2, DEVICES, 2, 128), BF16),
        pltpu.VMEM((ROWS, H * NB), BF16),
        pltpu.VMEM((ROWS, K), F32),
        pltpu.VMEM((256, 256), BF16),
        pltpu.VMEM((CL // BLK, NNB, BLK, WIN), BF16),
        pltpu.VMEM((CL, 2 * PAIRS), BF16),
        pltpu.VMEM((ROWS, CL), F32),
        pltpu.VMEM((ROWS, 2 * PAIRS), BF16),
        pltpu.VMEM((128, 512), BF16),
        pltpu.VMEM((2, NNB, EXT, NB), BF16),
        pltpu.VMEM((NNB, CL, NB), F32),
        pltpu.VMEM((CL, NB), F32),
        pltpu.VMEM((2, 2, ROWS // 2, 2, 128), BF16),
        pltpu.VMEM((2, 2, PAIRS // 2, 2, 128), BF16),
        pltpu.SemaphoreType.DMA((10,)),
        pltpu.SemaphoreType.DMA((NQ,)),
        pltpu.SemaphoreType.DMA((NQ,)),
        pltpu.SemaphoreType.DMA((2,)),
        pltpu.SemaphoreType.DMA((2,)),
        pltpu.SemaphoreType.DMA((2, 2)),
        pltpu.SemaphoreType.DMA((2, 2)),
    ]
    return pl.pallas_call(
        kernel,
        out_shape=pltpu.VMEM((2, CL, NB), F32),
        in_specs=[pl.BlockSpec(memory_space=pltpu.HBM)] * len(args),
        out_specs=pl.BlockSpec(memory_space=pltpu.VMEM),
        scratch_shapes=scratch,
        compiler_params=pltpu.CompilerParams(
            collective_id=0, has_side_effects=True, vmem_limit_bytes=48 << 20
        ),
        cost_estimate=pl.CostEstimate(
            flops=4_000_000_000, bytes_accessed=14 << 20, transcendentals=0
        ),
    )(*[pltpu.with_memory_space_constraint(a, pltpu.HBM) for a in args])


def solution(mesh):
    both = ("group", "member")
    in_specs = (
        P(both, None, None),
        P(),
        P(),
        P(),
        P(),
        P(),
        P(None, both, None),
        P(both, None),
        P(both, None, None),
        P(both, None, None),
        P(both, None, None, None),
    )
    out_specs = P(None, both, None)
    return jax.shard_map(body, mesh=mesh, in_specs=in_specs, out_specs=out_specs, check_vma=False)
```
